512 devices in a mesh: seq: 16 (over z), section: 8 (over x, core), dp: 4 (over y).
Axes of the slice: x: 4, y: 4, z: 16, core: 2. Of those that a mesh axis runs over, the one named last changes fastest.
Arguments:
- queries: bfloat16 [8, 4, 2048, 4096], P('section', 'dp', 'seq'), may hold values from -160 to 160
- keys: bfloat16 [8, 4, 2048, 512], P('section', 'dp', 'seq'), may hold values from -6 to 6
- output_gradient: bfloat16 [8, 4, 2048, 4096], P('section', 'dp', 'seq'), may hold values from -6 to 6
- rollout_index: int32 [8, 4, 2048], P('section', 'dp'), may hold values from 0 to 15, never falling along the last dimension, each value on 1 to 384 neighbouring positions
- loss_token_mask: int32 [8, 4, 2048], P('section', 'dp'), may hold values 0 or 1
- advantages: float32 [8, 4, 16], P('section', 'dp'), may hold values from -4 to 4
- value_projection: bfloat16 [8, 8192, 512], P('section', ('seq', 'dp')), may hold values from -0.25 to 0.25
- adapter_down_weight: bfloat16 [8, 8192, 64], P('section', ('seq', 'dp')), may hold values from -0.75 to 0.75
- adapter_up_weight: bfloat16 [8, 64, 512], P('section'), may hold values from -0.25 to 0.25
- adapter_activation: bfloat16 [8, 4, 2048, 64], P('section', 'dp', 'seq'), may hold values from -6 to 6
Outputs:
- handed: bfloat16 [8, 4, 2048, 8192], P('section', 'dp', 'seq')
- adapter_up_gradient: float32 [8, 64, 512], P('section', ('seq', 'dp'))
The draws below stay inside these ranges and needn't reach their ends.
Inputs may be any that keep to these rules, and one draw needn't show every extreme that they name: `rollout_index`: each rollout's tokens form one run; at most 384 tokens a rollout.
All inputs are finite; a program needn't handle non-finite values. No bound on the sum of `loss_token_mask` on one device may be relied on, other than what follows from the above.
Results may differ from the reference program's by a relative error of at most 0.015.
Values may be sent and summed in bfloat16 or wider, within the bound.
No kernel may reach another device: no remote copies, remote signals or barrier semaphores. Data moves between devices by JAX's collectives and lax.ppermute only.
A program may use at most 128 MiB of HBM per device.

```python
import math
import jax
import jax.numpy as jnp
import numpy as np
from jax import lax

MODEL_WIDTH = 8192
QUERY_HEAD_COUNT = 32
KEY_VALUE_HEADS = 4
HEAD_SIZE = 128
ADAPTER_RANK = 64
SECTION_TOTAL = 8
REPLICA_TOTAL = 4
SEQUENCE_LENGTH = 2048
SEGS = 16
MOST = 384


def shared_keys(key):
    return jnp.clip(jax.random.normal(key, (SECTION_TOTAL, REPLICA_TOTAL, SEQUENCE_LENGTH, KEY_VALUE_HEADS * HEAD_SIZE), jnp.float32), -5.0, 5.0)


def draw_keys(key, part):
    random_base_keys = shared_keys(key)
    return random_base_keys.astype(jnp.bfloat16)


def draw_queries(key, part):
    key = jax.random.fold_in(key, 12)
    key_fresh = jax.random.fold_in(key, 0)
    shape_all = (SECTION_TOTAL, REPLICA_TOTAL, SEQUENCE_LENGTH, QUERY_HEAD_COUNT * HEAD_SIZE)
    fresh = jax.random.normal(key_fresh, shape_all, jnp.float32)
    return jnp.clip(fresh, -160.0, 160.0).astype(jnp.bfloat16)


def touch_ends(array, own_key, smallest, top_value):
    spot = [jax.random.randint(jax.random.fold_in(own_key, axis), (), 0, length) for axis, length in enumerate(array.shape)]
    longest = array.shape.index(max(array.shape))
    beside = spot[:longest] + [(spot[longest] + 1) % array.shape[longest]] + spot[longest + 1:]
    return array.at[tuple(spot)].set(smallest).at[tuple(beside)].set(top_value)


def strengthened(drawn, key, source, target, blocks, factor):
    def block_of(dim):
        return (jnp.arange(drawn.shape[dim]) // (drawn.shape[dim] // blocks)).reshape((-1,) + (1,) * (drawn.ndim - 1 - dim))

    first = jax.random.permutation(key, blocks)[block_of(target)]
    far = (block_of(target) + blocks // 2) % blocks
    return jnp.where((block_of(source) == first) | (block_of(source) == far), factor * drawn, drawn)


def block_scale(key, shape, shards, low, largest):
    def one(axis_at, shards_of):
        steps = jax.random.uniform(jax.random.fold_in(jax.random.fold_in(key, 6), axis_at), (shards_of,), jnp.float32, low / len(shards), largest / len(shards))
        return jnp.repeat(jnp.exp(steps), shape[axis_at] // shards_of).reshape((-1,) + (1,) * (len(shape) - axis_at - 1))

    loudness = one(*shards[0])
    for cut in shards[1:]:
        loudness = loudness * one(*cut)
    return loudness


def split_up(count, total, bound, lean):
    portions = [(1 << 20) // math.isqrt(standing ** lean) + 1 for standing in range(2, count + 1)]
    surplus, holding = total - bound - (count - 1), [1] * (count - 1)
    while surplus > 0:
        movable = [i for i in range(count - 1) if holding[i] < bound]
        mass, budget = sum([portions[i] for i in movable]), surplus
        for i in movable:
            extra = min(bound - holding[i], max(1, budget * portions[i] // mass), surplus)
            holding[i] = holding[i] + extra
            surplus = surplus - extra
    return np.array([bound] + holding)


def ragged_sizes(rng, count, total, bound, slope):
    if count == 2:
        one = jax.random.randint(rng, (), max(1, total - bound), min(bound, total - 1) + 1)
        return jnp.stack([one, total - one])
    tallies = jnp.asarray(split_up(count, total, bound, slope), jnp.int32)
    pairs = (count - 1) // 2
    donor, taker = tallies[1:1 + 2 * pairs:2], tallies[2:2 + 2 * pairs:2]
    slack = jnp.minimum(donor - 1, bound - taker)
    moved = jax.random.randint(jax.random.fold_in(rng, 1), (pairs,), 0, 1 << 20) % (slack + 1)
    tallies = tallies.at[1:1 + 2 * pairs:2].set(donor - moved).at[2:2 + 2 * pairs:2].set(taker + moved)
    return tallies[jax.random.permutation(jax.random.fold_in(rng, 2), count)]


def normal_values(own_key, shape, spread, bound, shards=(), held_as=jnp.bfloat16):
    gain = block_scale(own_key, shape, shards, -0.22, 0.18) if shards else 1.0
    array = jax.random.normal(own_key, shape, jnp.float32) * spread * gain
    return jnp.minimum(jnp.maximum(array, -bound), bound).astype(held_as)


def noise_with(rng, dims, spread, reach, cuts, heavy, held_as=jnp.bfloat16):
    values = spread * jax.random.normal(rng, dims, jnp.float32)
    if cuts:
        values = values * block_scale(rng, dims, cuts, -0.22, 0.18)
    return jnp.clip(strengthened(values, jax.random.fold_in(rng, 3), *heavy), -reach, reach).astype(held_as)


def setup_inputs(seed: int = 0) -> dict:
    key_of = jax.random.split(jax.random.key(seed), 11)
    return {
        "queries": draw_queries(jax.random.fold_in(key_of[10], 71), 0),
        "keys": draw_keys(jax.random.fold_in(key_of[10], 71), 0),
        "output_gradient": normal_values(key_of[2], (SECTION_TOTAL, REPLICA_TOTAL, SEQUENCE_LENGTH, QUERY_HEAD_COUNT * HEAD_SIZE), 1.0, 6.0, ((0, 8), (1, 4), (2, 16))),
        "rollout_index": jax.vmap(lambda own: jnp.searchsorted(jnp.cumsum(ragged_sizes(own, SEGS, SEQUENCE_LENGTH, MOST, 1)), jnp.arange(SEQUENCE_LENGTH), side="right"))(jax.random.split(key_of[3], SECTION_TOTAL * REPLICA_TOTAL)).reshape((SECTION_TOTAL, REPLICA_TOTAL, SEQUENCE_LENGTH)).astype(jnp.int32),
        "loss_token_mask": touch_ends((jax.random.randint(key_of[4], (SECTION_TOTAL, REPLICA_TOTAL, SEQUENCE_LENGTH), 0, 4) < 3).astype(jnp.int32), jax.random.fold_in(key_of[4], 1), 0, 1),
        "advantages": normal_values(key_of[5], (SECTION_TOTAL, REPLICA_TOTAL, SEGS), 1.0, 4.0, ((0, 8), (1, 4)), jnp.float32),
        "value_projection": normal_values(key_of[6], (SECTION_TOTAL, MODEL_WIDTH, KEY_VALUE_HEADS * HEAD_SIZE), (KEY_VALUE_HEADS * HEAD_SIZE) ** -0.5, 0.25, ((0, 8), (1, 64))),
        "adapter_down_weight": normal_values(key_of[7], (SECTION_TOTAL, MODEL_WIDTH, ADAPTER_RANK), ADAPTER_RANK ** -0.5, 0.75, ((0, 8), (1, 64))),
        "adapter_up_weight": normal_values(key_of[8], (SECTION_TOTAL, ADAPTER_RANK, KEY_VALUE_HEADS * HEAD_SIZE), (KEY_VALUE_HEADS * HEAD_SIZE) ** -0.5, 0.25, ((0, 8),)),
        "adapter_activation": noise_with(key_of[9], (SECTION_TOTAL, REPLICA_TOTAL, SEQUENCE_LENGTH, ADAPTER_RANK), 1.0, 6.0, ((0, 8), (1, 4), (2, 16)), (2, 3, 16, 2.0)),
    }


def token_weights(rollout_row, token_mask_row, advantage_values):
    onehot = (rollout_row[:, None] == jnp.arange(SEGS, dtype=jnp.int32)[None, :]).astype(jnp.float32)
    return jnp.sum(onehot * advantage_values[None, :], axis=1) * token_mask_row.astype(jnp.float32)


def single_sequence(query_row_list, random_key_rows, gradient_rows, rollout_row, token_mask_row, advantage_values, value_projection, adapter_down_weight, adapter_up_weight, adapter_activation):
    weights = token_weights(rollout_row, token_mask_row, advantage_values)
    scaled_grad = (gradient_rows.astype(jnp.float32) * weights[:, None]).astype(jnp.bfloat16)
    positions = jnp.arange(SEQUENCE_LENGTH, dtype=jnp.int32)
    allowed = (positions[None, :] <= positions[:, None]) & (rollout_row[None, :] == rollout_row[:, None])
    query_group_size = QUERY_HEAD_COUNT // KEY_VALUE_HEADS

    def one_head(head):
        query_cols = lax.dynamic_slice_in_dim(query_row_list, head * HEAD_SIZE, HEAD_SIZE, 1)
        key_cols = lax.dynamic_slice_in_dim(random_key_rows, (head // query_group_size) * HEAD_SIZE, HEAD_SIZE, 1)
        grad_cols = lax.dynamic_slice_in_dim(scaled_grad, head * HEAD_SIZE, HEAD_SIZE, 1)
        scores = jnp.dot(query_cols, key_cols.T, preferred_element_type=jnp.float32) * (HEAD_SIZE ** -0.5)
        scores = jnp.where(allowed, scores, -1e30)
        row_max = jnp.max(scores, axis=1, keepdims=True)
        exp_terms = jnp.where(allowed, jnp.exp(scores - row_max), 0.0)
        prob_bf = (exp_terms / jnp.sum(exp_terms, axis=1, keepdims=True)).astype(jnp.bfloat16)
        return jnp.dot(prob_bf.T, grad_cols, preferred_element_type=jnp.float32)

    head_split = lax.map(one_head, jnp.arange(QUERY_HEAD_COUNT, dtype=jnp.int32))
    grouped_heads = jnp.sum(head_split.reshape(KEY_VALUE_HEADS, query_group_size, SEQUENCE_LENGTH, HEAD_SIZE), axis=1)
    value_gradient = grouped_heads.transpose(1, 0, 2).reshape(SEQUENCE_LENGTH, KEY_VALUE_HEADS * HEAD_SIZE).astype(jnp.bfloat16)
    adapter_middle = jnp.dot(value_gradient, adapter_up_weight.T, preferred_element_type=jnp.float32).astype(jnp.bfloat16)
    layer_gradient = (jnp.dot(value_gradient, value_projection.T, preferred_element_type=jnp.float32)
                  + jnp.dot(adapter_middle, adapter_down_weight.T, preferred_element_type=jnp.float32)).astype(jnp.bfloat16)
    adapter_term = jnp.dot(adapter_activation.T, value_gradient, preferred_element_type=jnp.float32)
    return layer_gradient, adapter_term


def reference(queries, keys, output_gradient, rollout_index, loss_token_mask, advantages, value_projection, adapter_down_weight, adapter_up_weight, adapter_activation):
    section_grads = []
    section_terms = []
    for section_position in range(SECTION_TOTAL):
        summed_total = jnp.zeros((ADAPTER_RANK, KEY_VALUE_HEADS * HEAD_SIZE), jnp.float32)
        row_list = []
        for replica_position in range(REPLICA_TOTAL):
            layer_gradient, adapter_term = single_sequence(
                queries[section_position, replica_position], keys[section_position, replica_position],
                output_gradient[section_position, replica_position], rollout_index[section_position, replica_position],
                loss_token_mask[section_position, replica_position], advantages[section_position, replica_position],
                value_projection[section_position], adapter_down_weight[section_position], adapter_up_weight[section_position],
                adapter_activation[section_position, replica_position])
            row_list.append(layer_gradient)
            summed_total = summed_total + adapter_term
        section_grads.append(jnp.stack(row_list))
        section_terms.append(summed_total)
    all_grads = jnp.stack(section_grads)
    handed = jnp.concatenate([all_grads[1:], jnp.zeros_like(all_grads[:1])], axis=0)
    return handed, jnp.stack(section_terms)
```

```python
import functools
import jax
import jax.numpy as jnp
from jax import lax
from jax.experimental import pallas as pl
from jax.experimental.pallas import tpu as pltpu
from jax.sharding import PartitionSpec as P

HEAD_SIZE = 128
LONGEST = 384
NEG_FILL = -1e30
SCORE_SCALE = HEAD_SIZE ** (-0.5) * 1.4426950408889634


def shifted(value, moves, cyclic=()):
    axes = tuple(moves)
    sizes = [lax.axis_size(axis) for axis in axes]
    pairs = []
    total = 1
    for size in sizes:
        total *= size
    for source in range(total):
        rest, coords = source, []
        for size in reversed(sizes):
            coords.append(rest % size)
            rest //= size
        coords.reverse()
        target, inside = 0, True
        for axis, size, at in zip(axes, sizes, coords):
            to = at + moves[axis]
            if axis in cyclic:
                to %= size
            inside = inside and 0 <= to < size
            target = target * size + to
        if inside:
            pairs.append((source, target))
    return lax.ppermute(value, axes if len(axes) > 1 else axes[0], pairs)


def attention_kernel(q_ref, g_ref, w_ref, bias_ref, *refs, chunks, heads):
    key_refs, out_refs = refs[:chunks], refs[chunks:]
    rows = q_ref.shape[0]
    keys = jnp.concatenate([ref[:rows] for ref in key_refs], axis=0)
    bias = bias_ref[...]
    bias2 = jnp.concatenate([bias, bias], axis=1)
    weight = w_ref[...]
    total = None
    for pair in range(heads // 2):
        cols = [slice((2 * pair + k) * HEAD_SIZE, (2 * pair + k + 1) * HEAD_SIZE) for k in (0, 1)]
        q2 = jnp.concatenate([q_ref[:, c] for c in cols], axis=0)
        g2 = jnp.concatenate(
            [(g_ref[:, c].astype(jnp.float32) * weight).astype(jnp.bfloat16) for c in cols], axis=0
        )
        scores = lax.dot_general(
            keys, q2, (((1,), (1,)), ((), ())), preferred_element_type=jnp.float32
        )
        scores = scores * SCORE_SCALE + bias2
        top = jnp.max(scores, axis=0, keepdims=True)
        terms = jnp.exp2(scores - top)
        inverse = 1.0 / jnp.sum(terms, axis=0, keepdims=True)
        probs = (terms * inverse).astype(jnp.bfloat16)
        part = jnp.dot(probs, g2, preferred_element_type=jnp.float32)
        total = part if total is None else total + part
    for index, ref in enumerate(out_refs):
        ref[...] = total[index * rows : (index + 1) * rows].astype(ref.dtype)


def attention(queries, grads, weight, bias, key_chunks):
    rows, width = queries.shape
    chunks = len(key_chunks)
    kv_heads = key_chunks[0].shape[1] // HEAD_SIZE
    group = width // kv_heads
    wide = pl.BlockSpec((rows, group), lambda i: (0, i))
    narrow = pl.BlockSpec((rows, HEAD_SIZE), lambda i: (0, i))
    keyed = pl.BlockSpec((key_chunks[0].shape[0], HEAD_SIZE), lambda i: (0, i))
    whole = lambda array: pl.BlockSpec(array.shape, lambda i: (0, 0))
    return pl.pallas_call(
        functools.partial(attention_kernel, chunks=chunks, heads=group // HEAD_SIZE),
        grid=(kv_heads,),
        in_specs=[wide, wide, whole(weight), whole(bias)] + [keyed] * chunks,
        out_specs=[narrow] * chunks,
        out_shape=[jax.ShapeDtypeStruct((rows, kv_heads * HEAD_SIZE), jnp.bfloat16)] * chunks,
        compiler_params=pltpu.CompilerParams(vmem_limit_bytes=32 * 1024 * 1024),
        cost_estimate=pl.CostEstimate(
            flops=4 * chunks * rows * rows * width,
            bytes_accessed=4 * rows * width,
            transcendentals=chunks * rows * rows * width // HEAD_SIZE,
        ),
    )(queries, grads, weight, bias, *key_chunks)


def packed_rows(array, width):
    bands = width // array.shape[1]
    rows = array.shape[0] // bands
    return jnp.concatenate([array[k * rows : (k + 1) * rows] for k in range(bands)], axis=1)


def prepare_kernel(keys_ref, act_ref, packed_ref):
    rows = keys_ref.shape[0]
    packed_ref[:rows] = keys_ref[...]
    packed_ref[rows:] = packed_rows(act_ref[...], keys_ref.shape[1])


def prepared(keys, act):
    extra = act.shape[0] * act.shape[1] // keys.shape[1]
    return pl.pallas_call(
        prepare_kernel,
        out_shape=jax.ShapeDtypeStruct((keys.shape[0] + extra, keys.shape[1]), keys.dtype),
        compiler_params=pltpu.CompilerParams(vmem_limit_bytes=32 * 1024 * 1024),
    )(keys, act)


def adapter_kernel(*refs, chunks):
    packed_refs, part_refs, out_ref = refs[:chunks], refs[chunks : 2 * chunks], refs[-1]
    members, count, width = out_ref.shape
    rank = members * count
    rows = part_refs[0].shape[0]
    act = jnp.concatenate(
        [
            ref[rows:, k * rank : (k + 1) * rank]
            for ref in packed_refs
            for k in range(width // rank)
        ],
        axis=0,
    )
    source = lax.broadcasted_iota(jnp.int32, (rank, rank), 0)
    target = lax.broadcasted_iota(jnp.int32, (rank, rank), 1)
    order = source == (target % count) * members + target // count
    order = order.astype(jnp.float32).astype(jnp.bfloat16)
    act = jnp.dot(act, order, preferred_element_type=jnp.float32).astype(jnp.bfloat16)
    parts = jnp.concatenate([ref[...] for ref in part_refs], axis=0)
    term = lax.dot_general(
        act, parts, (((0,), (0,)), ((), ())), preferred_element_type=jnp.float32
    )
    out_ref[...] = term.astype(out_ref.dtype).reshape(members, count, width)


def adapter_terms(packed_chunks, parts, members, seq_count):
    return pl.pallas_call(
        functools.partial(adapter_kernel, chunks=len(parts)),
        out_shape=jax.ShapeDtypeStruct((members, seq_count, parts[0].shape[1]), parts[0].dtype),
        compiler_params=pltpu.CompilerParams(vmem_limit_bytes=32 * 1024 * 1024),
    )(*packed_chunks, *parts)


def summed_kernel(*refs):
    part_refs, terms_ref, out_ref = refs[:-2], refs[-2], refs[-1]
    rows = part_refs[0].shape[0]
    total = part_refs[0][...].astype(jnp.float32)
    for ref in part_refs[1:]:
        total = total + ref[...].astype(jnp.float32)
    total = total.astype(out_ref.dtype)
    for member in range(out_ref.shape[0]):
        out_ref[member, :rows] = total
        out_ref[member, rows:] = terms_ref[member]


def summed_copies(parts, terms):
    rows, width = parts[0].shape
    members, extra, _ = terms.shape
    return pl.pallas_call(
        summed_kernel,
        out_shape=jax.ShapeDtypeStruct((members, rows + extra, width), parts[0].dtype),
        compiler_params=pltpu.CompilerParams(vmem_limit_bytes=32 * 1024 * 1024),
    )(*parts, terms)


def stacked_kernel(*refs):
    out_ref, start = refs[-1], 0
    for ref in refs[:-1]:
        out_ref[start : start + ref.shape[0]] = ref[...]
        start += ref.shape[0]


def stacked(arrays):
    rows = sum(array.shape[0] for array in arrays)
    return pl.pallas_call(
        stacked_kernel,
        out_shape=jax.ShapeDtypeStruct((rows, arrays[0].shape[1]), arrays[0].dtype),
        compiler_params=pltpu.CompilerParams(vmem_limit_bytes=32 * 1024 * 1024),
    )(*arrays)


def product_kernel(at_ref, grads_ref, *refs, distances, count):
    weight_refs, out_ref = refs[:-1], refs[-1]
    members, _, width = grads_ref.shape
    _, _, rows, block_rows = out_ref.shape
    grads = grads_ref[:, :rows].reshape(members * rows, width)
    at = at_ref[0]
    for ref, own in zip(weight_refs, distances):
        for first in range(0, len(own), 2):
            weights = ref[first * block_rows : (first + 2) * block_rows, :]
            values = lax.dot_general(
                grads, weights, (((1,), (1,)), ((), ())), preferred_element_type=jnp.float32
            ).astype(out_ref.dtype)
            for k in (0, 1):
                block = lax.rem(at + own[first + k], count)
                part = values[:, k * block_rows : (k + 1) * block_rows]
                out_ref[:, block] = part.reshape(members, rows, block_rows)


def products(at, grads, weights, distances, rows, block_rows, count):
    members = grads.shape[0]
    vmem = pl.BlockSpec(memory_space=pltpu.VMEM)
    return pl.pallas_call(
        functools.partial(product_kernel, distances=distances, count=count),
        in_specs=[pl.BlockSpec(memory_space=pltpu.SMEM)] + [vmem] * (1 + len(weights)),
        out_specs=vmem,
        out_shape=jax.ShapeDtypeStruct((members, count, rows, block_rows), grads.dtype),
        compiler_params=pltpu.CompilerParams(vmem_limit_bytes=48 * 1024 * 1024),
    )(at, grads, *weights)


def ordered_kernel(in_ref, out_ref):
    members, blocks, _, size = in_ref.shape
    for block in range(blocks):
        for member in range(members):
            at = (block * members + member) * size
            out_ref[:, at : at + size] = in_ref[member, block]


def ordered(exchanged):
    members, count, rows, size = exchanged.shape
    blocks = 2
    return pl.pallas_call(
        ordered_kernel,
        grid=(count // blocks,),
        in_specs=[pl.BlockSpec((members, blocks, rows, size), lambda i: (0, i, 0, 0))],
        out_specs=pl.BlockSpec((rows, blocks * members * size), lambda i: (0, i)),
        out_shape=jax.ShapeDtypeStruct((rows, count * members * size), exchanged.dtype),
        compiler_params=pltpu.CompilerParams(vmem_limit_bytes=32 * 1024 * 1024),
    )(exchanged)


def swapped(value, axis, bit):
    pairs = [(at, at ^ bit) for at in range(lax.axis_size(axis))]
    return lax.ppermute(value, axis, pairs)


def tied(values, others):
    return lax.optimization_barrier((values, others))[0]


def local(
    queries,
    keys,
    output_gradient,
    rollout_index,
    loss_token_mask,
    advantages,
    value_projection,
    adapter_down_weight,
    adapter_up_weight,
    adapter_activation,
):
    seq_at = lax.axis_index("seq")
    seq_count = lax.axis_size("seq")
    dp_count = lax.axis_size("dp")
    rows = queries.shape[2]
    rank = adapter_activation.shape[3]
    halo = min(-(-(LONGEST - 1) // rows), seq_count - 1)
    ring = functools.partial(shifted, cyclic=("seq",))

    packed = prepared(keys[0, 0], adapter_activation[0, 0])
    chunks = [shifted(packed, {"seq": d}) for d in range(halo, 0, -1)] + [packed]

    merged = (
        value_projection[0].astype(jnp.float32)
        + jnp.dot(adapter_down_weight[0], adapter_up_weight[0], preferred_element_type=jnp.float32)
    ).astype(jnp.bfloat16)
    block_rows = merged.shape[0]
    high4 = ring(merged, {"seq": -4, "section": -1})
    low4 = ring(merged, {"seq": 4, "section": -1})
    own = shifted(merged, {"section": -1})

    rollout_row = rollout_index[0, 0]
    start = seq_at * rows
    padded = jnp.concatenate([jnp.full((halo * rows,), -1, jnp.int32), rollout_row])
    window = lax.dynamic_slice_in_dim(padded, start, (halo + 1) * rows, 0)
    own_rollout = window[halo * rows :]
    own_mask = lax.dynamic_slice_in_dim(loss_token_mask[0, 0], start, rows, 0)
    advantage_values = advantages[0, 0]
    onehot = (
        own_rollout[:, None] == jnp.arange(advantage_values.shape[0], dtype=jnp.int32)[None, :]
    ).astype(jnp.float32)
    weight = jnp.sum(onehot * advantage_values[None, :], axis=1) * own_mask.astype(jnp.float32)
    weight = jnp.broadcast_to(weight[:, None], (rows, HEAD_SIZE))
    key_pos = jnp.arange((halo + 1) * rows, dtype=jnp.int32)
    row_pos = jnp.arange(rows, dtype=jnp.int32) + halo * rows
    allowed = (key_pos[:, None] <= row_pos[None, :]) & (window[:, None] == own_rollout[None, :])
    bias = jnp.where(allowed, 0.0, NEG_FILL).astype(jnp.float32)

    parts = attention(queries[0, 0], output_gradient[0, 0], weight, bias, chunks)

    returned = [
        shifted(part, {"seq": index - halo, "section": -1} if index < halo else {"section": -1})
        for index, part in enumerate(parts)
    ]
    terms = adapter_terms(chunks, parts, dp_count, seq_count)

    high4 = tied(high4, parts)
    far = ring(high4, {"seq": -4})
    far = tied(far, returned[-1])
    fours = stacked([own, high4, far, low4])
    before = ring(fours, {"seq": 1})
    after = ring(fours, {"seq": -1})
    two_before = ring(fours[: 2 * block_rows], {"seq": 2})
    two_after = ring(fours[block_rows : 3 * block_rows], {"seq": -2})

    copies = summed_copies(returned, terms)
    grads = lax.all_to_all(copies, "dp", split_axis=0, concat_axis=0, tiled=True)
    product = products(
        seq_at.astype(jnp.int32).reshape(1),
        grads,
        [fours, before, after, two_before, two_after],
        [(0, 4, 8, 12), (15, 3, 7, 11), (1, 5, 9, 13), (14, 2), (6, 10)],
        rows,
        block_rows,
        seq_count,
    )
    exchanged = lax.all_to_all(product, "dp", split_axis=0, concat_axis=0, tiled=True)
    handed = ordered(exchanged)

    term = jnp.sum(grads[:, rows:].astype(jnp.float32), axis=0)
    term = tied(term, product)
    bit = 1
    while bit < seq_count:
        term = term + swapped(term, "seq", bit)
        bit *= 2
    term = lax.dynamic_slice_in_dim(term, seq_at, 1, 0)
    return (handed[None, None], term[None])


def solution(mesh):
    placed = (
        P("section", "dp", "seq", None),
        P("section", "dp", "seq", None),
        P("section", "dp", "seq", None),
        P("section", "dp", None),
        P("section", "dp", None),
        P("section", "dp", None),
        P("section", ("seq", "dp"), None),
        P("section", ("seq", "dp"), None),
        P("section", None, None),
        P("section", "dp", "seq", None),
    )
    return jax.shard_map(
        local,
        mesh=mesh,
        in_specs=placed,
        out_specs=(P("section", "dp", "seq", None), P("section", ("seq", "dp"), None)),
        check_vma=False,
    )
```

```python
import functools
import jax
import jax.numpy as jnp
from jax import lax
from jax.experimental import pallas as pl
from jax.experimental.pallas import tpu as pltpu
from jax.sharding import PartitionSpec as P

HEAD_SIZE = 128
LONGEST = 384
NEG_FILL = -1e30
SCORE_SCALE = HEAD_SIZE ** (-0.5) * 1.4426950408889634


def shifted(value, moves, cyclic=()):
    axes = tuple(moves)
    sizes = [lax.axis_size(axis) for axis in axes]
    pairs = []
    total = 1
    for size in sizes:
        total *= size
    for source in range(total):
        rest, coords = source, []
        for size in reversed(sizes):
            coords.append(rest % size)
            rest //= size
        coords.reverse()
        target, inside = 0, True
        for axis, size, at in zip(axes, sizes, coords):
            to = at + moves[axis]
            if axis in cyclic:
                to %= size
            inside = inside and 0 <= to < size
            target = target * size + to
        if inside:
            pairs.append((source, target))
    return lax.ppermute(value, axes if len(axes) > 1 else axes[0], pairs)


def attention_kernel(q_ref, g_ref, w_ref, bias_ref, *refs, chunks, heads):
    key_refs, out_refs = refs[:chunks], refs[chunks:]
    rows = q_ref.shape[0]
    keys = jnp.concatenate([ref[:rows] for ref in key_refs], axis=0)
    bias = bias_ref[...]
    bias2 = jnp.concatenate([bias, bias], axis=1)
    weight = w_ref[...]
    total = None
    for pair in range(heads // 2):
        cols = [slice((2 * pair + k) * HEAD_SIZE, (2 * pair + k + 1) * HEAD_SIZE) for k in (0, 1)]
        q2 = jnp.concatenate([q_ref[:, c] for c in cols], axis=0)
        g2 = jnp.concatenate(
            [(g_ref[:, c].astype(jnp.float32) * weight).astype(jnp.bfloat16) for c in cols], axis=0
        )
        scores = lax.dot_general(
            keys, q2, (((1,), (1,)), ((), ())), preferred_element_type=jnp.float32
        )
        scores = scores * SCORE_SCALE + bias2
        top = jnp.max(scores, axis=0, keepdims=True)
        terms = jnp.exp2(scores - top)
        inverse = 1.0 / jnp.sum(terms, axis=0, keepdims=True)
        probs = (terms * inverse).astype(jnp.bfloat16)
        part = jnp.dot(probs, g2, preferred_element_type=jnp.float32)
        total = part if total is None else total + part
    for index, ref in enumerate(out_refs):
        ref[...] = total[index * rows : (index + 1) * rows].astype(ref.dtype)


def attention(queries, grads, weight, bias, key_chunks):
    rows, width = queries.shape
    chunks = len(key_chunks)
    kv_heads = key_chunks[0].shape[1] // HEAD_SIZE
    group = width // kv_heads
    wide = pl.BlockSpec((rows, group), lambda i: (0, i))
    narrow = pl.BlockSpec((rows, HEAD_SIZE), lambda i: (0, i))
    keyed = pl.BlockSpec((key_chunks[0].shape[0], HEAD_SIZE), lambda i: (0, i))
    whole = lambda array: pl.BlockSpec(array.shape, lambda i: (0, 0))
    return pl.pallas_call(
        functools.partial(attention_kernel, chunks=chunks, heads=group // HEAD_SIZE),
        grid=(kv_heads,),
        in_specs=[wide, wide, whole(weight), whole(bias)] + [keyed] * chunks,
        out_specs=[narrow] * chunks,
        out_shape=[jax.ShapeDtypeStruct((rows, kv_heads * HEAD_SIZE), jnp.bfloat16)] * chunks,
        compiler_params=pltpu.CompilerParams(vmem_limit_bytes=32 * 1024 * 1024),
        cost_estimate=pl.CostEstimate(
            flops=4 * chunks * rows * rows * width,
            bytes_accessed=4 * rows * width,
            transcendentals=chunks * rows * rows * width // HEAD_SIZE,
        ),
    )(queries, grads, weight, bias, *key_chunks)


def packed_rows(array, width):
    bands = width // array.shape[1]
    rows = array.shape[0] // bands
    return jnp.concatenate([array[k * rows : (k + 1) * rows] for k in range(bands)], axis=1)


def prepare_kernel(keys_ref, act_ref, packed_ref):
    rows = keys_ref.shape[0]
    packed_ref[:rows] = keys_ref[...]
    packed_ref[rows:] = packed_rows(act_ref[...], keys_ref.shape[1])


def prepared(keys, act):
    extra = act.shape[0] * act.shape[1] // keys.shape[1]
    return pl.pallas_call(
        prepare_kernel,
        out_shape=jax.ShapeDtypeStruct((keys.shape[0] + extra, keys.shape[1]), keys.dtype),
        compiler_params=pltpu.CompilerParams(vmem_limit_bytes=32 * 1024 * 1024),
    )(keys, act)


def adapter_kernel(*refs, chunks):
    packed_refs, part_refs, out_ref = refs[:chunks], refs[chunks : 2 * chunks], refs[-1]
    members, count, width = out_ref.shape
    rank = members * count
    rows = part_refs[0].shape[0]
    act = jnp.concatenate(
        [
            ref[rows:, k * rank : (k + 1) * rank]
            for ref in packed_refs
            for k in range(width // rank)
        ],
        axis=0,
    )
    source = lax.broadcasted_iota(jnp.int32, (rank, rank), 0)
    target = lax.broadcasted_iota(jnp.int32, (rank, rank), 1)
    order = source == (target % count) * members + target // count
    order = order.astype(jnp.float32).astype(jnp.bfloat16)
    act = jnp.dot(act, order, preferred_element_type=jnp.float32).astype(jnp.bfloat16)
    parts = jnp.concatenate([ref[...] for ref in part_refs], axis=0)
    term = lax.dot_general(
        act, parts, (((0,), (0,)), ((), ())), preferred_element_type=jnp.float32
    )
    out_ref[...] = term.astype(out_ref.dtype).reshape(members, count, width)


def adapter_terms(packed_chunks, parts, members, seq_count):
    return pl.pallas_call(
        functools.partial(adapter_kernel, chunks=len(parts)),
        out_shape=jax.ShapeDtypeStruct((members, seq_count, parts[0].shape[1]), parts[0].dtype),
        compiler_params=pltpu.CompilerParams(vmem_limit_bytes=32 * 1024 * 1024),
    )(*packed_chunks, *parts)


def summed_kernel(*refs):
    part_refs, terms_ref, out_ref = refs[:-2], refs[-2], refs[-1]
    rows = part_refs[0].shape[0]
    total = part_refs[0][...].astype(jnp.float32)
    for ref in part_refs[1:]:
        total = total + ref[...].astype(jnp.float32)
    total = total.astype(out_ref.dtype)
    for member in range(out_ref.shape[0]):
        out_ref[member, :rows] = total
        out_ref[member, rows:] = terms_ref[member]


def summed_copies(parts, terms):
    rows, width = parts[0].shape
    members, extra, _ = terms.shape
    return pl.pallas_call(
        summed_kernel,
        out_shape=jax.ShapeDtypeStruct((members, rows + extra, width), parts[0].dtype),
        compiler_params=pltpu.CompilerParams(vmem_limit_bytes=32 * 1024 * 1024),
    )(*parts, terms)


def stacked_kernel(*refs):
    out_ref, start = refs[-1], 0
    for ref in refs[:-1]:
        out_ref[start : start + ref.shape[0]] = ref[...]
        start += ref.shape[0]


def stacked(arrays):
    rows = sum(array.shape[0] for array in arrays)
    return pl.pallas_call(
        stacked_kernel,
        out_shape=jax.ShapeDtypeStruct((rows, arrays[0].shape[1]), arrays[0].dtype),
        compiler_params=pltpu.CompilerParams(vmem_limit_bytes=32 * 1024 * 1024),
    )(*arrays)


def product_kernel(grads_ref, *refs):
    weight_refs, out_ref = refs[:-1], refs[-1]
    members, _, width = grads_ref.shape
    _, _, rows, block_rows = out_ref.shape
    grads = grads_ref[:, :rows].reshape(members * rows, width)
    block = 0
    for ref in weight_refs:
        values = lax.dot_general(
            grads, ref[...], (((1,), (1,)), ((), ())), preferred_element_type=jnp.float32
        ).astype(out_ref.dtype)
        for k in range(ref.shape[0] // block_rows):
            part = values[:, k * block_rows : (k + 1) * block_rows]
            out_ref[:, block] = part.reshape(members, rows, block_rows)
            block += 1


def products(grads, weights, rows, block_rows):
    blocks = sum(weight.shape[0] for weight in weights) // block_rows
    return pl.pallas_call(
        product_kernel,
        out_shape=jax.ShapeDtypeStruct((grads.shape[0], blocks, rows, block_rows), grads.dtype),
        compiler_params=pltpu.CompilerParams(vmem_limit_bytes=48 * 1024 * 1024),
    )(grads, *weights)


def placed_kernel(places_ref, in_ref, *refs):
    out_ref = refs[-1]
    members, _, _, size = in_ref.shape
    for member in range(members):
        out_ref[:, member * size : (member + 1) * size] = in_ref[member, 0]


def placed_blocks(exchanged, places, count, before=None):
    members, blocks, rows, size = exchanged.shape
    operands = [exchanged] + ([] if before is None else [before])
    return pl.pallas_call(
        placed_kernel,
        grid_spec=pltpu.PrefetchScalarGridSpec(
            num_scalar_prefetch=1,
            grid=(blocks,),
            in_specs=[pl.BlockSpec((members, 1, rows, size), lambda i, places: (0, i, 0, 0))]
            + ([] if before is None else [pl.BlockSpec(memory_space=pl.ANY)]),
            out_specs=pl.BlockSpec((rows, members * size), lambda i, places: (0, places[i])),
        ),
        out_shape=jax.ShapeDtypeStruct((rows, count * members * size), exchanged.dtype),
        input_output_aliases={} if before is None else {2: 0},
        compiler_params=pltpu.CompilerParams(vmem_limit_bytes=32 * 1024 * 1024),
    )(places, *operands)


def term_kernel(grads_ref, out_ref):
    total = grads_ref[0].astype(jnp.float32)
    for member in range(1, grads_ref.shape[0]):
        total = total + grads_ref[member].astype(jnp.float32)
    out_ref[...] = total


def summed_terms(grads, rows):
    members, total, width = grads.shape
    extra = total - rows
    return pl.pallas_call(
        term_kernel,
        grid=(1,),
        in_specs=[pl.BlockSpec((members, extra, width), lambda i: (0, rows // extra, 0))],
        out_specs=pl.BlockSpec((extra, width), lambda i: (0, 0)),
        out_shape=jax.ShapeDtypeStruct((extra, width), jnp.float32),
        compiler_params=pltpu.CompilerParams(vmem_limit_bytes=32 * 1024 * 1024),
    )(grads)


def tied(values, others):
    return lax.optimization_barrier((values, others))[0]


def local(
    queries,
    keys,
    output_gradient,
    rollout_index,
    loss_token_mask,
    advantages,
    value_projection,
    adapter_down_weight,
    adapter_up_weight,
    adapter_activation,
):
    seq_at = lax.axis_index("seq")
    seq_count = lax.axis_size("seq")
    dp_count = lax.axis_size("dp")
    rows = queries.shape[2]
    rank = adapter_activation.shape[3]
    halo = min(-(-(LONGEST - 1) // rows), seq_count - 1)
    ring = functools.partial(shifted, cyclic=("seq",))

    packed = prepared(keys[0, 0], adapter_activation[0, 0])
    chunks = [shifted(packed, {"seq": d}) for d in range(halo, 0, -1)] + [packed]

    merged = (
        value_projection[0].astype(jnp.float32)
        + jnp.dot(adapter_down_weight[0], adapter_up_weight[0], preferred_element_type=jnp.float32)
    ).astype(jnp.bfloat16)
    block_rows = merged.shape[0]
    merged = tied(merged, chunks[2])
    high4 = ring(merged, {"seq": -4, "section": -1})
    low4 = ring(merged, {"seq": 4, "section": -1})
    own = shifted(merged, {"section": -1})

    rollout_row = rollout_index[0, 0]
    start = seq_at * rows
    padded = jnp.concatenate([jnp.full((halo * rows,), -1, jnp.int32), rollout_row])
    window = lax.dynamic_slice_in_dim(padded, start, (halo + 1) * rows, 0)
    own_rollout = window[halo * rows :]
    own_mask = lax.dynamic_slice_in_dim(loss_token_mask[0, 0], start, rows, 0)
    advantage_values = advantages[0, 0]
    onehot = (
        own_rollout[:, None] == jnp.arange(advantage_values.shape[0], dtype=jnp.int32)[None, :]
    ).astype(jnp.float32)
    weight = jnp.sum(onehot * advantage_values[None, :], axis=1) * own_mask.astype(jnp.float32)
    weight = jnp.broadcast_to(weight[:, None], (rows, HEAD_SIZE))
    key_pos = jnp.arange((halo + 1) * rows, dtype=jnp.int32)
    row_pos = jnp.arange(rows, dtype=jnp.int32) + halo * rows
    allowed = (key_pos[:, None] <= row_pos[None, :]) & (window[:, None] == own_rollout[None, :])
    bias = jnp.where(allowed, 0.0, NEG_FILL).astype(jnp.float32)

    parts = attention(queries[0, 0], output_gradient[0, 0], weight, bias, chunks)

    returned = [
        shifted(part, {"seq": index - halo, "section": -1} if index < halo else {"section": -1})
        for index, part in enumerate(parts)
    ]
    terms = adapter_terms(chunks, parts, dp_count, seq_count)

    high4, low4, own = tied([high4, low4, own], parts)
    half = block_rows // 2
    far = [ring(low4[:half], {"seq": 4}), ring(high4[half:], {"seq": -4})]
    far = tied(far, returned[-1])
    held = stacked([own, high4] + far + [low4])
    before = ring(held, {"seq": 1})
    after = ring(held, {"seq": -1})
    two_before = ring(before[: 2 * block_rows], {"seq": 1})
    two_after = ring(after[block_rows : 3 * block_rows], {"seq": -1})

    copies = summed_copies(returned, terms)
    grads = lax.all_to_all(copies, "dp", split_axis=0, concat_axis=0, tiled=True)
    term = summed_terms(grads, rows)
    term = term.reshape(seq_count, 1, -1)
    term = lax.all_to_all(term, "seq", split_axis=0, concat_axis=0, tiled=True)
    term = jnp.sum(term, axis=0)

    def exchanged(weights):
        return lax.all_to_all(
            products(grads, weights, rows, block_rows), "dp", split_axis=0, concat_axis=0, tiled=True
        )

    def places(*distances):
        return (seq_at.astype(jnp.int32) + jnp.array(distances, jnp.int32)) % seq_count

    first = exchanged([held, before, after])
    second = exchanged([two_before, two_after])
    handed = placed_blocks(first, places(0, 4, 8, 12, 15, 3, 7, 11, 1, 5, 9, 13), seq_count)
    handed = placed_blocks(second, places(14, 2, 6, 10), seq_count, handed)
    return (handed[None, None], term[None])


def solution(mesh):
    placed = (
        P("section", "dp", "seq", None),
        P("section", "dp", "seq", None),
        P("section", "dp", "seq", None),
        P("section", "dp", None),
        P("section", "dp", None),
        P("section", "dp", None),
        P("section", ("seq", "dp"), None),
        P("section", ("seq", "dp"), None),
        P("section", None, None),
        P("section", "dp", "seq", None),
    )
    return jax.shard_map(
        local,
        mesh=mesh,
        in_specs=placed,
        out_specs=(P("section", "dp", "seq", None), P("section", ("seq", "dp"), None)),
        check_vma=False,
    )
```

```python
import functools
import jax
import jax.numpy as jnp
from jax import lax
from jax.experimental import pallas as pl
from jax.experimental.pallas import tpu as pltpu
from jax.sharding import PartitionSpec as P

HEAD_SIZE = 128
LONGEST = 384
NEG_FILL = -1e30
SCORE_SCALE = HEAD_SIZE ** (-0.5) * 1.4426950408889634


def shifted(value, moves, cyclic=()):
    axes = tuple(moves)
    sizes = [lax.axis_size(axis) for axis in axes]
    pairs = []
    total = 1
    for size in sizes:
        total *= size
    for source in range(total):
        rest, coords = source, []
        for size in reversed(sizes):
            coords.append(rest % size)
            rest //= size
        coords.reverse()
        target, inside = 0, True
        for axis, size, at in zip(axes, sizes, coords):
            to = at + moves[axis]
            if axis in cyclic:
                to %= size
            inside = inside and 0 <= to < size
            target = target * size + to
        if inside:
            pairs.append((source, target))
    return lax.ppermute(value, axes if len(axes) > 1 else axes[0], pairs)


def attention_kernel(q_ref, g_ref, w_ref, bias_ref, *refs, chunks, heads):
    key_refs, out_refs = refs[:chunks], refs[chunks:]
    rows = q_ref.shape[0]
    keys = jnp.concatenate([ref[:rows] for ref in key_refs], axis=0)
    bias = bias_ref[...]
    bias2 = jnp.concatenate([bias, bias], axis=1)
    weight = w_ref[...]
    total = None
    for pair in range(heads // 2):
        cols = [slice((2 * pair + k) * HEAD_SIZE, (2 * pair + k + 1) * HEAD_SIZE) for k in (0, 1)]
        q2 = jnp.concatenate([q_ref[:, c] for c in cols], axis=0)
        g2 = jnp.concatenate(
            [(g_ref[:, c].astype(jnp.float32) * weight).astype(jnp.bfloat16) for c in cols], axis=0
        )
        scores = lax.dot_general(
            keys, q2, (((1,), (1,)), ((), ())), preferred_element_type=jnp.float32
        )
        scores = scores * SCORE_SCALE + bias2
        top = jnp.max(scores, axis=0, keepdims=True)
        terms = jnp.exp2(scores - top)
        inverse = 1.0 / jnp.sum(terms, axis=0, keepdims=True)
        probs = (terms * inverse).astype(jnp.bfloat16)
        part = jnp.dot(probs, g2, preferred_element_type=jnp.float32)
        total = part if total is None else total + part
    for index, ref in enumerate(out_refs):
        ref[...] = total[index * rows : (index + 1) * rows].astype(ref.dtype)


def attention(queries, grads, weight, bias, key_chunks):
    rows, width = queries.shape
    chunks = len(key_chunks)
    kv_heads = key_chunks[0].shape[1] // HEAD_SIZE
    group = width // kv_heads
    wide = pl.BlockSpec((rows, group), lambda i: (0, i))
    narrow = pl.BlockSpec((rows, HEAD_SIZE), lambda i: (0, i))
    keyed = pl.BlockSpec((key_chunks[0].shape[0], HEAD_SIZE), lambda i: (0, i))
    whole = lambda array: pl.BlockSpec(array.shape, lambda i: (0, 0))
    return pl.pallas_call(
        functools.partial(attention_kernel, chunks=chunks, heads=group // HEAD_SIZE),
        grid=(kv_heads,),
        in_specs=[wide, wide, whole(weight), whole(bias)] + [keyed] * chunks,
        out_specs=[narrow] * chunks,
        out_shape=[jax.ShapeDtypeStruct((rows, kv_heads * HEAD_SIZE), jnp.bfloat16)] * chunks,
        compiler_params=pltpu.CompilerParams(vmem_limit_bytes=32 * 1024 * 1024),
        cost_estimate=pl.CostEstimate(
            flops=4 * chunks * rows * rows * width,
            bytes_accessed=4 * rows * width,
            transcendentals=chunks * rows * rows * width // HEAD_SIZE,
        ),
    )(queries, grads, weight, bias, *key_chunks)


def packed_rows(array, width):
    bands = width // array.shape[1]
    rows = array.shape[0] // bands
    return jnp.concatenate([array[k * rows : (k + 1) * rows] for k in range(bands)], axis=1)


def prepare_kernel(keys_ref, act_ref, packed_ref):
    rows = keys_ref.shape[0]
    packed_ref[:rows] = keys_ref[...]
    packed_ref[rows:] = packed_rows(act_ref[...], keys_ref.shape[1])


def prepared(keys, act):
    extra = act.shape[0] * act.shape[1] // keys.shape[1]
    return pl.pallas_call(
        prepare_kernel,
        out_shape=jax.ShapeDtypeStruct((keys.shape[0] + extra, keys.shape[1]), keys.dtype),
        compiler_params=pltpu.CompilerParams(vmem_limit_bytes=32 * 1024 * 1024),
    )(keys, act)


def adapter_kernel(*refs, chunks):
    packed_refs, part_refs, out_ref = refs[:chunks], refs[chunks : 2 * chunks], refs[-1]
    members, count, width = out_ref.shape
    rank = members * count
    rows = part_refs[0].shape[0]
    act = jnp.concatenate(
        [
            ref[rows:, k * rank : (k + 1) * rank]
            for ref in packed_refs
            for k in range(width // rank)
        ],
        axis=0,
    )
    source = lax.broadcasted_iota(jnp.int32, (rank, rank), 0)
    target = lax.broadcasted_iota(jnp.int32, (rank, rank), 1)
    order = source == (target % count) * members + target // count
    order = order.astype(jnp.float32).astype(jnp.bfloat16)
    act = jnp.dot(act, order, preferred_element_type=jnp.float32).astype(jnp.bfloat16)
    parts = jnp.concatenate([ref[...] for ref in part_refs], axis=0)
    term = lax.dot_general(
        act, parts, (((0,), (0,)), ((), ())), preferred_element_type=jnp.float32
    )
    out_ref[...] = term.astype(out_ref.dtype).reshape(members, count, width)


def adapter_terms(packed_chunks, parts, members, seq_count):
    return pl.pallas_call(
        functools.partial(adapter_kernel, chunks=len(parts)),
        out_shape=jax.ShapeDtypeStruct((members, seq_count, parts[0].shape[1]), parts[0].dtype),
        compiler_params=pltpu.CompilerParams(vmem_limit_bytes=32 * 1024 * 1024),
    )(*packed_chunks, *parts)


def summed_kernel(*refs):
    part_refs, terms_ref, out_ref = refs[:-2], refs[-2], refs[-1]
    rows = part_refs[0].shape[0]
    total = part_refs[0][...].astype(jnp.float32)
    for ref in part_refs[1:]:
        total = total + ref[...].astype(jnp.float32)
    total = total.astype(out_ref.dtype)
    for member in range(out_ref.shape[0]):
        out_ref[member, :rows] = total
        out_ref[member, rows:] = terms_ref[member]


def summed_copies(parts, terms):
    rows, width = parts[0].shape
    members, extra, _ = terms.shape
    return pl.pallas_call(
        summed_kernel,
        out_shape=jax.ShapeDtypeStruct((members, rows + extra, width), parts[0].dtype),
        compiler_params=pltpu.CompilerParams(vmem_limit_bytes=32 * 1024 * 1024),
    )(*parts, terms)


def stacked_kernel(*refs):
    out_ref, start = refs[-1], 0
    for ref in refs[:-1]:
        out_ref[start : start + ref.shape[0]] = ref[...]
        start += ref.shape[0]


def stacked(arrays):
    rows = sum(array.shape[0] for array in arrays)
    return pl.pallas_call(
        stacked_kernel,
        out_shape=jax.ShapeDtypeStruct((rows, arrays[0].shape[1]), arrays[0].dtype),
        compiler_params=pltpu.CompilerParams(vmem_limit_bytes=32 * 1024 * 1024),
    )(*arrays)


def product_kernel(grads_ref, *refs, weights):
    weight_refs, out_refs = refs[:weights], refs[weights:]
    members, _, width = grads_ref.shape
    rows, block_rows = out_refs[0].shape[-2:]
    grads = grads_ref[:, :rows].reshape(members * rows, width)
    block = 0
    for ref in weight_refs:
        values = lax.dot_general(
            grads, ref[...], (((1,), (1,)), ((), ())), preferred_element_type=jnp.float32
        ).astype(out_refs[0].dtype)
        for k in range(ref.shape[0] // block_rows):
            part = values[:, k * block_rows : (k + 1) * block_rows]
            out_refs[0][:, block] = part.reshape(members, rows, block_rows)
            block += 1


def products(grads, weights, rows, block_rows):
    blocks = sum(weight.shape[0] for weight in weights) // block_rows
    return pl.pallas_call(
        functools.partial(product_kernel, weights=len(weights)),
        out_shape=jax.ShapeDtypeStruct((grads.shape[0], blocks, rows, block_rows), grads.dtype),
        compiler_params=pltpu.CompilerParams(vmem_limit_bytes=48 * 1024 * 1024),
    )(grads, *weights)


def placed_kernel(members_ref, places_ref, *refs, count):
    part_refs, out_ref, sems = refs[:count], refs[-2], refs[-1]
    blocks, _, size = part_refs[0].shape
    copies = []
    for block in range(blocks):
        for index, ref in enumerate(part_refs):
            at = pl.multiple_of((places_ref[block] * count + members_ref[index]) * size, size)
            copy = pltpu.make_async_copy(
                ref.at[block], out_ref.at[:, pl.ds(at, size)], sems.at[block, index]
            )
            copy.start()
            copies.append(copy)
    for copy in copies:
        copy.wait()


def placed_parts(parts, members, places, width, before=None):
    blocks, rows, _ = parts[0].shape
    anywhere = pl.BlockSpec(memory_space=pl.ANY)
    scalar = pl.BlockSpec(memory_space=pltpu.SMEM)
    operands = list(parts) + ([] if before is None else [before])
    return pl.pallas_call(
        functools.partial(placed_kernel, count=len(parts)),
        in_specs=[scalar, scalar] + [anywhere] * len(operands),
        out_specs=anywhere,
        out_shape=jax.ShapeDtypeStruct((rows, width), parts[0].dtype),
        input_output_aliases={} if before is None else {2 + len(parts): 0},
        scratch_shapes=[pltpu.SemaphoreType.DMA((blocks, len(parts)))],
        compiler_params=pltpu.CompilerParams(vmem_limit_bytes=32 * 1024 * 1024),
    )(members, places, *operands)


def placed_whole_kernel(places_ref, in_ref, *refs):
    out_ref, sems = refs[-2], refs[-1]
    members, blocks, _, size = in_ref.shape
    copies = []
    for block in range(blocks):
        for member in range(members):
            at = pl.multiple_of((places_ref[block] * members + member) * size, size)
            copy = pltpu.make_async_copy(
                in_ref.at[member, block], out_ref.at[:, pl.ds(at, size)], sems.at[block, member]
            )
            copy.start()
            copies.append(copy)
    for copy in copies:
        copy.wait()


def placed_whole(exchanged, places, width, before=None):
    members, blocks, rows, _ = exchanged.shape
    anywhere = pl.BlockSpec(memory_space=pl.ANY)
    operands = [exchanged] + ([] if before is None else [before])
    return pl.pallas_call(
        placed_whole_kernel,
        in_specs=[pl.BlockSpec(memory_space=pltpu.SMEM)] + [anywhere] * len(operands),
        out_specs=anywhere,
        out_shape=jax.ShapeDtypeStruct((rows, width), exchanged.dtype),
        input_output_aliases={} if before is None else {2: 0},
        scratch_shapes=[pltpu.SemaphoreType.DMA((blocks, members))],
        compiler_params=pltpu.CompilerParams(vmem_limit_bytes=32 * 1024 * 1024),
    )(places, *operands)


def term_kernel(grads_ref, out_ref):
    total = grads_ref[0].astype(jnp.float32)
    for member in range(1, grads_ref.shape[0]):
        total = total + grads_ref[member].astype(jnp.float32)
    out_ref[...] = total


def summed_terms(grads, rows):
    members, total, width = grads.shape
    extra = total - rows
    return pl.pallas_call(
        term_kernel,
        grid=(1,),
        in_specs=[pl.BlockSpec((members, extra, width), lambda i: (0, rows // extra, 0))],
        out_specs=pl.BlockSpec((extra, width), lambda i: (0, 0)),
        out_shape=jax.ShapeDtypeStruct((extra, width), jnp.float32),
        compiler_params=pltpu.CompilerParams(vmem_limit_bytes=32 * 1024 * 1024),
    )(grads)


def tied(values, others):
    return lax.optimization_barrier((values, others))[0]


def local(
    queries,
    keys,
    output_gradient,
    rollout_index,
    loss_token_mask,
    advantages,
    value_projection,
    adapter_down_weight,
    adapter_up_weight,
    adapter_activation,
):
    seq_at = lax.axis_index("seq")
    seq_count = lax.axis_size("seq")
    dp_count = lax.axis_size("dp")
    rows = queries.shape[2]
    rank = adapter_activation.shape[3]
    halo = min(-(-(LONGEST - 1) // rows), seq_count - 1)
    ring = functools.partial(shifted, cyclic=("seq",))

    packed = prepared(keys[0, 0], adapter_activation[0, 0])
    chunks = [shifted(packed, {"seq": d}) for d in range(halo, 0, -1)] + [packed]

    merged = (
        value_projection[0].astype(jnp.float32)
        + jnp.dot(adapter_down_weight[0], adapter_up_weight[0], preferred_element_type=jnp.float32)
    ).astype(jnp.bfloat16)
    block_rows = merged.shape[0]
    merged = tied(merged, chunks[2])
    high4 = ring(merged, {"seq": -4, "section": -1})
    low4 = ring(merged, {"seq": 4, "section": -1})
    own = shifted(merged, {"section": -1})

    rollout_row = rollout_index[0, 0]
    start = seq_at * rows
    padded = jnp.concatenate([jnp.full((halo * rows,), -1, jnp.int32), rollout_row])
    window = lax.dynamic_slice_in_dim(padded, start, (halo + 1) * rows, 0)
    own_rollout = window[halo * rows :]
    own_mask = lax.dynamic_slice_in_dim(loss_token_mask[0, 0], start, rows, 0)
    advantage_values = advantages[0, 0]
    onehot = (
        own_rollout[:, None] == jnp.arange(advantage_values.shape[0], dtype=jnp.int32)[None, :]
    ).astype(jnp.float32)
    weight = jnp.sum(onehot * advantage_values[None, :], axis=1) * own_mask.astype(jnp.float32)
    weight = jnp.broadcast_to(weight[:, None], (rows, HEAD_SIZE))
    key_pos = jnp.arange((halo + 1) * rows, dtype=jnp.int32)
    row_pos = jnp.arange(rows, dtype=jnp.int32) + halo * rows
    allowed = (key_pos[:, None] <= row_pos[None, :]) & (window[:, None] == own_rollout[None, :])
    bias = jnp.where(allowed, 0.0, NEG_FILL).astype(jnp.float32)

    parts = attention(queries[0, 0], output_gradient[0, 0], weight, bias, chunks)

    returned = [
        shifted(part, {"seq": index - halo, "section": -1} if index < halo else {"section": -1})
        for index, part in enumerate(parts)
    ]
    terms = adapter_terms(chunks, parts, dp_count, seq_count)

    high4, low4, own = tied([high4, low4, own], parts)
    half = block_rows // 2
    far = [ring(low4[:half], {"seq": 4}), ring(high4[half:], {"seq": -4})]
    far = tied(far, returned[-1])
    held = stacked([own, high4] + far + [low4])
    before = ring(held, {"seq": 1})
    after = ring(held, {"seq": -1})
    two_before = ring(before[: 2 * block_rows], {"seq": 1})
    two_after = ring(after[block_rows : 3 * block_rows], {"seq": -1})

    copies = summed_copies(returned, terms)
    grads = lax.all_to_all(copies, "dp", split_axis=0, concat_axis=0, tiled=True)
    term = summed_terms(grads, rows)
    term = term.reshape(seq_count, 1, -1)
    term = lax.all_to_all(term, "seq", split_axis=0, concat_axis=0, tiled=True)
    term = jnp.sum(term, axis=0)

    def exchanged(weights):
        return lax.all_to_all(
            products(grads, weights, rows, block_rows), "dp", split_axis=0, concat_axis=0, tiled=True
        )

    def passed(weights):
        product = products(grads, weights, rows, block_rows)
        parts = []
        for step in range(dp_count):
            at = (dp_at + step) % dp_count
            part = lax.dynamic_index_in_dim(product, at, 0, keepdims=False)
            parts.append(shifted(part, {"dp": step}, cyclic=("dp",)) if step else part)
        return parts

    def places(*distances):
        return (seq_at.astype(jnp.int32) + jnp.array(distances, jnp.int32)) % seq_count

    dp_at = lax.axis_index("dp").astype(jnp.int32)
    members = (dp_at - jnp.arange(dp_count, dtype=jnp.int32)) % dp_count
    width = seq_count * dp_count * block_rows
    first_places = places(0, 4, 8, 12, 15, 3, 7, 11, 1, 5, 9, 13)
    second_places = places(14, 2, 6, 10)
    first = exchanged([held, before, after])
    handed = placed_whole(first, first_places, width)
    second = exchanged([two_before, two_after])
    handed = placed_whole(second, second_places, width, handed)
    return (handed[None, None], term[None])


def solution(mesh):
    placed = (
        P("section", "dp", "seq", None),
        P("section", "dp", "seq", None),
        P("section", "dp", "seq", None),
        P("section", "dp", None),
        P("section", "dp", None),
        P("section", "dp", None),
        P("section", ("seq", "dp"), None),
        P("section", ("seq", "dp"), None),
        P("section", None, None),
        P("section", "dp", "seq", None),
    )
    return jax.shard_map(
        local,
        mesh=mesh,
        in_specs=placed,
        out_specs=(P("section", "dp", "seq", None), P("section", ("seq", "dp"), None)),
        check_vma=False,
    )
```
